32 devices in a mesh: row: 4 (over y, x), col: 2 (over core), depth: 4 (over z).
Axes of the slice: x: 2, y: 2, z: 4, core: 2. Of those that a mesh axis runs over, the one named last changes fastest.
Arguments:
- integrals: float32 [8, 6144, 4096], P(('col', 'depth'), 'row'), may hold values from -0.0546875 to 0.0546875
- amplitudes: float32 [8, 256, 4096], P('col', ('row', 'depth')), may hold values from -6 to 6
- block_list: int32 [8, 4], P('col'), may hold values from -1 to 7, as said below
- pair_list: int32 [256, 2], replicated, may hold values from 0 to 15, as said below
Outputs:
- residual: float32 [256, 6144], P(None, ('row', 'col', 'depth'))
The draws below stay inside these ranges and needn't reach their ends.
Inputs may be any that keep to these rules, and one draw needn't show every extreme that they name: `block_list`: slot s belongs to summation index s // 4; a live entry names a column block b with b // 4 equal to that index. The live slots of one row block and one summation index name distinct blocks, between 2 and 4 of them, lying anywhere among its 4 slots; in every draw some row block and index have exactly 4. `pair_list`: the rows are all 16 x 16 ordered pairs (i, j), each once, in a drawn order.
All inputs are finite; a program needn't handle non-finite values.
Results may differ from the reference program's by a relative error of at most 0.0003.
Values sent between devices are 32-bit elements; how exact they have to be, the bound alone decides.
A program may use at most 128 MiB of HBM per device.

```python
import jax
import jax.numpy as jnp
from jax import lax

BLOCK = 4096
NOCC = 16
PAIRS = 256
SLOT_COL = 4
BLK_DEV = 4
RB = 1536
NRB = 4
ROWS = 6144
SLOTS = 8
NCB = 8


def draw_block_list(key, part):
    key = jax.random.fold_in(key, 11)
    col_count = NCB // BLK_DEV
    key_count, key_pick, key_rank, key_block = jax.random.split(key, 4)
    counts = jax.random.randint(key_count, (NRB * col_count,), 2, BLK_DEV + 1)
    picked = jax.random.randint(key_pick, (), 0, NRB * col_count)
    counts = jnp.where(jnp.arange(NRB * col_count) == picked, BLK_DEV, counts).reshape(NRB, col_count)
    rank_keys = jax.random.split(key_rank, NRB * col_count)
    ranks = jax.vmap(lambda sub: jax.random.permutation(sub, SLOT_COL))(rank_keys).reshape(NRB, col_count, SLOT_COL)
    block_keys = jax.random.split(key_block, NRB * col_count)
    orders = jax.vmap(lambda sub: jax.random.permutation(sub, BLK_DEV))(block_keys).reshape(NRB, col_count, BLK_DEV)
    chosen = jnp.take_along_axis(orders, jnp.clip(ranks, 0, BLK_DEV - 1), axis=2)
    owners = jnp.arange(col_count).reshape(1, col_count, 1) * BLK_DEV
    living = ranks < counts[:, :, None]
    idents = jnp.where(living, owners + chosen, -1)
    return jnp.transpose(idents, (1, 2, 0)).reshape(SLOTS, NRB).astype(jnp.int32)


def draw_pair_list(key, part):
    key = jax.random.fold_in(key, 23)
    codes = jax.random.permutation(key, PAIRS)
    return jnp.stack([codes // NOCC, codes % NOCC], axis=1).astype(jnp.int32)


def level_of(own_key, shape, cuts, low, high):
    loudness = 1.0
    for axis_at, blocks in cuts:
        draws = jax.random.uniform(jax.random.fold_in(jax.random.fold_in(own_key, 6), axis_at), (blocks,), jnp.float32, low / len(cuts), high / len(cuts))
        loudness = loudness * jnp.repeat(jnp.exp(draws), shape[axis_at] // blocks).reshape((-1,) + (1,) * (len(shape) - 1 - axis_at))
    return loudness


def scatter_about(own_key, dims, spread, bound, cuts=(), held_as=jnp.bfloat16):
    array = spread * jax.random.normal(own_key, dims, jnp.float32)
    if cuts:
        array = array * level_of(own_key, dims, cuts, -0.22, 0.18)
    return jnp.clip(array, -bound, bound).astype(held_as)


def setup_inputs(seed: int = 0) -> dict:
    key_list = jax.random.split(jax.random.key(seed), 5)
    return {
        "integrals": scatter_about(key_list[0], (SLOTS, ROWS, BLOCK), (3 * BLOCK) ** -0.5, 0.0546875, ((0, 8), (1, 4)), jnp.float32),
        "amplitudes": scatter_about(key_list[1], (NCB, PAIRS, BLOCK), 1.0, 6.0, ((0, 2), (1, 16)), jnp.float32),
        "block_list": draw_block_list(jax.random.fold_in(key_list[4], 71), 0),
        "pair_list": draw_pair_list(jax.random.fold_in(key_list[4], 71), 0),
    }


def slot_product(chosen, slab_rows):
    return lax.dot_general(chosen, slab_rows, (((1,), (1,)), ((), ())), precision=lax.Precision.HIGHEST, preferred_element_type=jnp.float32)


def reference(integrals, amplitudes, block_list, pair_list):
    pieces = []
    for row_block in range(NRB):
        rows_here = integrals[:, row_block * RB:(row_block + 1) * RB, :]
        ident_list = block_list[:, row_block]

        def advance(accum, inputs):
            slab_rows, ident = inputs
            chosen = lax.dynamic_index_in_dim(amplitudes, jnp.maximum(ident, 0).astype(jnp.int32), 0, keepdims=False)
            grown = lax.cond(ident >= 0, lambda acc: acc + slot_product(chosen, slab_rows), lambda acc: acc, accum)
            return grown, None

        start_acc = jnp.zeros((PAIRS, RB), jnp.float32)
        ladder_block, _ = lax.scan(advance, start_acc, (rows_here, ident_list))
        pieces.append(ladder_block)
    ladder = jnp.concatenate(pieces, axis=1)
    codes = (pair_list[:, 0] * NOCC + pair_list[:, 1]).astype(jnp.int32)
    mirror_codes = (pair_list[:, 1] * NOCC + pair_list[:, 0]).astype(jnp.int32)
    positions = jnp.zeros((PAIRS,), jnp.int32).at[codes].set(jnp.arange(PAIRS, dtype=jnp.int32))
    mirror = positions[mirror_codes]
    return ladder + ladder[mirror]
```

```python
import functools

import jax
import jax.numpy as jnp
from jax import lax
from jax.experimental import pallas as pl
from jax.experimental.pallas import tpu as pltpu
from jax.sharding import PartitionSpec as P

F32 = jnp.float32
BF16 = jnp.bfloat16
CHUNK = 128
NT = (((1,), (1,)), ((), ()))


def split2(value):
    high = value.astype(BF16)
    return high, (value - high.astype(F32)).astype(BF16)


def dot(lhs, rhs):
    return jnp.dot(lhs, rhs, preferred_element_type=F32)


def ladder_kernel(
    nr, nc, nd,
    codes_all, codes_plane, blocks, amp, integ, out,
    slab, raw, joint, staged, chosen, acc, got_col, got_depth, mask_in, mask_ext,
    slab_sem, first_send, first_recv, line_send, line_recv, plane_send, plane_recv,
    col_send, col_recv, depth_send, depth_recv,
):
    r = lax.axis_index("row")
    c = lax.axis_index("col")
    d = lax.axis_index("depth")
    nblk, own_pairs, width = amp.shape
    quarter = width // nr
    steps = quarter // CHUNK
    plane_pairs = nr * own_pairs
    sym = out.shape[0]
    share = out.shape[1]

    def remote(src, dst, send, recv, **to):
        return pltpu.make_async_remote_copy(
            src_ref=src, dst_ref=dst, send_sem=send, recv_sem=recv,
            device_id=to, device_id_type=pl.DeviceIdType.MESH,
        )

    inner = jnp.logical_and(d >= 1, d <= 2)
    outer = jnp.logical_or(d == 0, d == 3)
    lower = d < 2
    ext = jnp.where(lower, 0, 3)
    mate = 3 - d
    inward = jnp.where(lower, d + 1, d - 1)
    outward = jnp.where(lower, 0, 3)

    barrier = pltpu.get_barrier_semaphore()
    for o in range(1, nr):
        pl.semaphore_signal(barrier, inc=1, device_id={"row": lax.rem(r + o, nr)},
                            device_id_type=pl.DeviceIdType.MESH)
    for o in range(1, nc):
        pl.semaphore_signal(barrier, inc=1, device_id={"col": lax.rem(c + o, nc)},
                            device_id_type=pl.DeviceIdType.MESH)
    for o in range(1, nd):
        pl.semaphore_signal(barrier, inc=1, device_id={"depth": lax.rem(d + o, nd)},
                            device_id_type=pl.DeviceIdType.MESH)
    pl.semaphore_wait(barrier, nr + nc + nd - 3)

    def first_copy(j, o):
        to = lax.rem(r + o, nr)
        at = pl.multiple_of(to * quarter + j * CHUNK, CHUNK)
        src = amp.at[:, :, pl.ds(at, CHUNK)]
        dst = raw.at[j, d, :, pl.ds(pl.multiple_of(r * own_pairs, own_pairs), own_pairs), :]
        if o == 0:
            return pltpu.make_async_copy(src, dst, first_recv.at[j, 0])
        return remote(src, dst, first_send.at[j, o], first_recv.at[j, o], row=to)

    def first_start(j, _):
        for o in range(nr):
            first_copy(j, o).start()
        return 0

    lax.fori_loop(0, steps, first_start, 0)
    slab_copy = pltpu.make_async_copy(integ.at[0], slab, slab_sem)
    slab_copy.start()

    def one_hot(codes):
        n = codes.shape[1]
        at = lax.broadcasted_iota(jnp.int32, (sym, n), 0)
        return jnp.where((codes >> 2) == at, codes & 3, 0).astype(F32)

    plane_of = lax.broadcasted_iota(jnp.int32, (sym, nd * plane_pairs), 1) // plane_pairs
    mask_in[...] = jnp.where(plane_of == ext, 0.0, one_hot(codes_all[...]))
    mask_ext[...] = one_hot(codes_plane[ext])
    acc[...] = jnp.zeros_like(acc)

    def own_copy(j):
        return remote(raw.at[j, d], raw.at[j, d], line_send.at[j, 0], line_recv.at[j, d], depth=inward)

    def forward_copy(j):
        return remote(raw.at[j, outward], raw.at[j, outward], line_send.at[j, 1],
                      line_recv.at[j, outward], depth=inward)

    def joint_copy(j):
        return remote(joint.at[j], joint.at[j], line_send.at[j, 2], line_recv.at[j, nd], depth=outward)

    def raw_arrived(j, z):
        remote(raw.at[j, z], raw.at[j, z], line_send.at[j, 0], line_recv.at[j, z], depth=inward).wait_recv()

    def plane_copy(j, o):
        to = lax.rem(r + o, nr)
        return remote(staged.at[j, o], chosen.at[j, r], plane_send.at[j, o], plane_recv.at[j, o], row=to)

    def spread(j):
        m_ext = mask_ext[...].astype(BF16)
        sums = []
        for b in range(nblk):
            high, low = split2(raw[j, ext, b])
            sums.append(joint[j, b] + (dot(m_ext, high) + dot(m_ext, low)))
        for o in range(nr):
            to = lax.rem(r + o, nr)
            at = lax.rem(jnp.maximum(blocks[d, to], 0), nblk)
            picked = sums[0]
            for b in range(1, nblk):
                picked = jnp.where(at == b, sums[b], picked)
            if o == 0:
                chosen[j, r] = picked
            else:
                staged[j, o] = picked
                plane_copy(j, o).start()

    def step(t, _):
        @pl.when(t < steps)
        def _():
            for o in range(nr):
                copy = first_copy(t, o)
                if o == 0:
                    copy.wait()
                else:
                    copy.wait_recv()
            own_copy(t).start()

        @pl.when(jnp.logical_and(inner, jnp.logical_and(t >= 1, t < steps + 1)))
        def _():
            raw_arrived(t - 1, outward)
            forward_copy(t - 1).start()

        @pl.when(jnp.logical_and(inner, jnp.logical_and(t >= 2, t < steps + 2)))
        def _():
            j = t - 2
            raw_arrived(j, mate)
            raw_arrived(j, 3 - outward)
            m_in = mask_in[...].astype(BF16)
            for b in range(nblk):
                high, low = split2(raw[j, :, b].reshape(nd * plane_pairs, CHUNK))
                joint[j, b] = dot(m_in, high) + dot(m_in, low)
            joint_copy(j).start()
            spread(j)

        @pl.when(jnp.logical_and(outer, jnp.logical_and(t >= 3, t < steps + 3)))
        def _():
            joint_copy(t - 3).wait_recv()
            spread(t - 3)

        @pl.when(t == 4)
        def _():
            slab_copy.wait()

        @pl.when(t >= 4)
        def _():
            j = t - 4
            for o in range(1, nr):
                plane_copy(j, o).wait_recv()
            lhs = jnp.concatenate([chosen[j, q] for q in range(nr)], axis=1)
            l_high, l_low = split2(lhs)

            def tile(s, _):
                rows = pl.ds(pl.multiple_of(s * share, 8), share)
                rhs = jnp.concatenate(
                    [slab[rows, pl.ds(pl.multiple_of(q * quarter + j * CHUNK, CHUNK), CHUNK)]
                     for q in range(nr)], axis=1)
                r_high, r_low = split2(rhs)
                value = lax.dot_general(l_high, r_high, NT, preferred_element_type=F32)
                value += lax.dot_general(l_high, r_low, NT, preferred_element_type=F32)
                value += lax.dot_general(l_low, r_high, NT, preferred_element_type=F32)
                acc[s // nd, lax.rem(s, nd)] += value
                return 0

            lax.fori_loop(0, nc * nd, tile, 0)

        return 0

    lax.fori_loop(0, steps + 4, step, 0)

    live = blocks[d, r] >= 0
    acc[...] = jnp.where(live, acc[...], 0.0)

    def col_copy(o):
        to = lax.rem(c + o, nc)
        return remote(acc.at[to], got_col.at[o], col_send.at[o], col_recv.at[o], col=to)

    for o in range(1, nc):
        col_copy(o).start()
    for o in range(1, nc):
        col_copy(o).wait_recv()
    total = acc[c]
    for o in range(1, nc):
        total += got_col[o]
    got_col[0] = total

    def depth_copy(o):
        to = lax.rem(d + o, nd)
        return remote(got_col.at[0, to], got_depth.at[o], depth_send.at[o], depth_recv.at[o], depth=to)

    for o in range(1, nd):
        depth_copy(o).start()
    for o in range(1, nd):
        depth_copy(o).wait_recv()
    total = got_col[0, d]
    for o in range(1, nd):
        total += got_depth[o]
    out[...] = total

    for o in range(1, nc):
        col_copy(o).wait_send()
    for o in range(1, nd):
        depth_copy(o).wait_send()

    def finish(j, _):
        for o in range(1, nr):
            first_copy(j, o).wait_send()
            plane_copy(j, o).wait_send()
        own_copy(j).wait_send()

        @pl.when(inner)
        def _():
            forward_copy(j).wait_send()
            joint_copy(j).wait_send()

        return 0

    lax.fori_loop(0, steps, finish, 0)


def per_device(mesh, integrals, amplitudes, block_list, pair_list):
    nr, nc, nd = mesh.shape["row"], mesh.shape["col"], mesh.shape["depth"]
    _, rows, width = integrals.shape
    nblk, own_pairs, _ = amplitudes.shape
    pairs = pair_list.shape[0]
    nocc = int(round(pairs ** 0.5))
    sym = nocc * (nocc + 1) // 2
    plane_pairs = nr * own_pairs
    share = rows // (nc * nd)
    steps = width // nr // CHUNK

    big = jnp.maximum(pair_list[:, 0], pair_list[:, 1])
    small = jnp.minimum(pair_list[:, 0], pair_list[:, 1])
    unordered = big * (big + 1) // 2 + small
    codes = unordered * 4 + jnp.where(big == small, 2, 1)
    codes = codes.reshape(nr, nd, own_pairs).transpose(1, 0, 2)
    codes_plane = codes.reshape(nd, 1, plane_pairs)
    codes_all = codes.reshape(1, pairs)

    dma = pltpu.SemaphoreType.DMA
    sums = pl.pallas_call(
        functools.partial(ladder_kernel, nr, nc, nd),
        out_shape=jax.ShapeDtypeStruct((sym, share), F32),
        in_specs=[
            pl.BlockSpec(memory_space=pltpu.VMEM),
            pl.BlockSpec(memory_space=pltpu.VMEM),
            pl.BlockSpec(memory_space=pltpu.SMEM),
            pl.BlockSpec(memory_space=pl.ANY),
            pl.BlockSpec(memory_space=pl.ANY),
        ],
        out_specs=pl.BlockSpec(memory_space=pltpu.VMEM),
        scratch_shapes=[
            pltpu.VMEM((rows, width), F32),
            pltpu.VMEM((steps, nd, nblk, plane_pairs, CHUNK), F32),
            pltpu.VMEM((steps, nblk, sym, CHUNK), F32),
            pltpu.VMEM((steps, nr, sym, CHUNK), F32),
            pltpu.VMEM((steps, nr, sym, CHUNK), F32),
            pltpu.VMEM((nc, nd, sym, share), F32),
            pltpu.VMEM((nc, nd, sym, share), F32),
            pltpu.VMEM((nd, sym, share), F32),
            pltpu.VMEM((sym, pairs), F32),
            pltpu.VMEM((sym, plane_pairs), F32),
            dma, dma((steps, nr)), dma((steps, nr)),
            dma((steps, 3)), dma((steps, nd + 1)),
            dma((steps, nr)), dma((steps, nr)),
            dma((nc,)), dma((nc,)), dma((nd,)), dma((nd,)),
        ],
        compiler_params=pltpu.CompilerParams(
            collective_id=0, has_side_effects=True, vmem_limit_bytes=56 * 1024 * 1024
        ),
        cost_estimate=pl.CostEstimate(
            flops=6 * sym * rows * width, bytes_accessed=4 * rows * width, transcendentals=0
        ),
    )(codes_all, codes_plane, block_list, amplitudes, integrals)

    expand = (unordered[:, None] == jnp.arange(sym)[None, :]).astype(F32)
    return jnp.dot(expand, sums, precision=lax.Precision.HIGHEST, preferred_element_type=F32)


def solution(mesh):
    return jax.shard_map(
        functools.partial(per_device, mesh),
        mesh=mesh,
        in_specs=(
            P(("col", "depth"), "row", None),
            P("col", ("row", "depth"), None),
            P("col", None),
            P(),
        ),
        out_specs=P(None, ("row", "col", "depth")),
        check_vma=False,
    )
```

```python
import functools

import jax
import jax.numpy as jnp
from jax import lax
from jax.experimental import pallas as pl
from jax.experimental.pallas import tpu as pltpu
from jax.sharding import PartitionSpec as P

F32 = jnp.float32
BF16 = jnp.bfloat16
CHUNK = 128
GROUPS = 1
JOINT_LAG = 1
OUTER_LAG = 3
PRODUCT_LAG = 4
NT = (((1,), (1,)), ((), ()))
TN = (((0,), (0,)), ((), ()))


def split2(value):
    high = value.astype(BF16)
    return high, (value - high.astype(F32)).astype(BF16)


def dot(lhs, rhs):
    return jnp.dot(lhs, rhs, preferred_element_type=F32)


def ladder_kernel(
    nr, nc, nd,
    pair_list, block_list, amp, integ, out,
    pairs, blocks, slab, raw, joint, staged, chosen, acc, got_col, got_depth, mask_in, mask_ext, spread_back,
    pair_sem, block_sem, slab_sem, first_send, first_recv, line_send, line_recv, plane_send, plane_recv,
    col_send, col_recv, depth_send, depth_recv,
):
    r = lax.axis_index("row")
    c = lax.axis_index("col")
    d = lax.axis_index("depth")
    nblk, own_pairs, width = amp.shape
    quarter = width // nr
    steps = quarter // CHUNK
    plane_pairs = nr * own_pairs
    sym = mask_in.shape[0]
    share = out.shape[0]
    units = steps * GROUPS
    per_group = nblk // GROUPS

    def remote(src, dst, send, recv, **to):
        return pltpu.make_async_remote_copy(
            src_ref=src, dst_ref=dst, send_sem=send, recv_sem=recv,
            device_id=to, device_id_type=pl.DeviceIdType.MESH,
        )

    inner = jnp.logical_and(d >= 1, d <= 2)
    outer = jnp.logical_or(d == 0, d == 3)
    lower = d < 2
    ext = jnp.where(lower, 0, 3)
    mate = 3 - d
    inward = jnp.where(lower, d + 1, d - 1)
    outward = jnp.where(lower, 0, 3)

    barrier = pltpu.get_barrier_semaphore()
    for o in range(1, nr):
        pl.semaphore_signal(barrier, inc=1, device_id={"row": lax.rem(r + o, nr)},
                            device_id_type=pl.DeviceIdType.MESH)
    for o in range(1, nc):
        pl.semaphore_signal(barrier, inc=1, device_id={"col": lax.rem(c + o, nc)},
                            device_id_type=pl.DeviceIdType.MESH)
    for o in range(1, nd):
        pl.semaphore_signal(barrier, inc=1, device_id={"depth": lax.rem(d + o, nd)},
                            device_id_type=pl.DeviceIdType.MESH)
    slab_copy = pltpu.make_async_copy(integ.at[0], slab, slab_sem)
    pair_copy = pltpu.make_async_copy(pair_list, pairs, pair_sem)
    block_copy = pltpu.make_async_copy(block_list, blocks, block_sem)
    pair_copy.start()
    block_copy.start()
    pl.semaphore_wait(barrier, nr + nc + nd - 3)

    def first_copy(j, o):
        to = lax.rem(r + o, nr)
        at = pl.multiple_of(to * quarter + j * CHUNK, CHUNK)
        src = amp.at[:, :, pl.ds(at, CHUNK)]
        dst = raw.at[j, d, :, pl.ds(pl.multiple_of(r * own_pairs, own_pairs), own_pairs), :]
        if o == 0:
            return pltpu.make_async_copy(src, dst, first_recv.at[j, 0])
        return remote(src, dst, first_send.at[j, o], first_recv.at[j, o], row=to)

    def first_start(j, _):
        for o in range(nr):
            first_copy(j, o).start()
        return 0

    lax.fori_loop(0, 1, first_start, 0)

    pair_copy.wait()
    block_copy.wait()
    first, second = pairs[0:1, :], pairs[1:2, :]
    big, small = jnp.maximum(first, second), jnp.minimum(first, second)
    n = nd * plane_pairs
    hit = ((big * (big + 1)) >> 1) + small == lax.broadcasted_iota(jnp.int32, (n, n), 0)
    spread_back[...] = jnp.where(hit, 1.0, 0.0)[:sym]
    weighted = jnp.where(hit, jnp.where(big == small, 2.0, 1.0), 0.0).T
    planes = []
    for z in range(nd):
        planes.append(jnp.concatenate(
            [weighted[(q * nd + z) * own_pairs:(q * nd + z + 1) * own_pairs] for q in range(nr)], axis=0))
    none = jnp.zeros_like(planes[0])
    first_plane = jnp.where(lower, none, planes[0])
    last_plane = jnp.where(lower, planes[3], none)
    mask_in[...] = jnp.concatenate([first_plane, planes[1], planes[2], last_plane], axis=0).T[:sym]
    mask_ext[...] = jnp.concatenate([jnp.where(lower, planes[0], planes[3]), none], axis=0).T[:sym, :plane_pairs]
    acc[...] = jnp.zeros_like(acc)

    def part(ref, u, *at):
        return ref.at[(u // GROUPS, *at, pl.ds(lax.rem(u, GROUPS) * per_group, per_group))]

    def own_copy(u):
        return remote(part(raw, u, d), part(raw, u, d), line_send.at[u, 0], line_recv.at[u, d], depth=inward)

    def forward_copy(u):
        return remote(part(raw, u, outward), part(raw, u, outward), line_send.at[u, 1],
                      line_recv.at[u, outward], depth=inward)

    def joint_copy(u):
        return remote(part(joint, u), part(joint, u), line_send.at[u, 2], line_recv.at[u, nd], depth=outward)

    def raw_arrived(u, z):
        remote(part(raw, u, z), part(raw, u, z), line_send.at[u, 0], line_recv.at[u, z], depth=inward).wait_recv()

    def plane_copy(j, o):
        to = lax.rem(r + o, nr)
        return remote(staged.at[j, o], chosen.at[j, r], plane_send.at[j, o], plane_recv.at[j, o], row=to)

    def spread(j):
        m_ext = mask_ext[...].astype(BF16)
        sums = []
        for b in range(0, nblk, 2):
            high, low = split2(jnp.concatenate([raw[j, ext, b], raw[j, ext, b + 1]], axis=1))
            value = dot(m_ext, high) + dot(m_ext, low)
            sums.append(joint[j, b] + value[:, :CHUNK])
            sums.append(joint[j, b + 1] + value[:, CHUNK:])
        for o in range(nr):
            to = lax.rem(r + o, nr)
            at = lax.rem(jnp.maximum(blocks[d, to], 0), nblk)
            picked = sums[0]
            for b in range(1, nblk):
                picked = jnp.where(at == b, sums[b], picked)
            if o == 0:
                chosen[j, r] = picked
            else:
                staged[j, o] = picked
                plane_copy(j, o).start()

    def step(t, _):
        @pl.when(t + 1 < steps)
        def _():
            first_start(t + 1, 0)

        @pl.when(t == 1)
        def _():
            slab_copy.start()

        @pl.when(t < units)
        def _():
            @pl.when(lax.rem(t, GROUPS) == 0)
            def _():
                for o in range(nr):
                    copy = first_copy(t // GROUPS, o)
                    if o == 0:
                        copy.wait()
                    else:
                        copy.wait_recv()

            own_copy(t).start()

        @pl.when(jnp.logical_and(inner, t < units))
        def _():
            raw_arrived(t, outward)
            forward_copy(t).start()

        @pl.when(jnp.logical_and(inner, jnp.logical_and(t >= JOINT_LAG, t < units + JOINT_LAG)))
        def _():
            u = t - JOINT_LAG
            j = u // GROUPS
            raw_arrived(u, mate)
            raw_arrived(u, 3 - outward)
            m_in = mask_in[...].astype(BF16)
            for k in range(0, per_group, 2):
                b = lax.rem(u, GROUPS) * per_group + k
                high, low = split2(jnp.concatenate(
                    [raw[j, :, b + e].reshape(nd * plane_pairs, CHUNK) for e in range(2)], axis=1))
                value = dot(m_in, high) + dot(m_in, low)
                joint[j, b] = value[:, :CHUNK]
                joint[j, b + 1] = value[:, CHUNK:]
            joint_copy(u).start()

            @pl.when(lax.rem(u, GROUPS) == GROUPS - 1)
            def _():
                spread(j)

        @pl.when(jnp.logical_and(outer, jnp.logical_and(t >= OUTER_LAG, t < units + OUTER_LAG)))
        def _():
            u = t - OUTER_LAG
            joint_copy(u).wait_recv()

            @pl.when(lax.rem(u, GROUPS) == GROUPS - 1)
            def _():
                spread(u // GROUPS)

        @pl.when(t == PRODUCT_LAG)
        def _():
            slab_copy.wait()

        @pl.when(jnp.logical_and(t >= PRODUCT_LAG, lax.rem(t - PRODUCT_LAG, GROUPS) == GROUPS - 1))
        def _():
            j = (t - PRODUCT_LAG) // GROUPS
            for o in range(1, nr):
                plane_copy(j, o).wait_recv()
            lhs = jnp.concatenate([chosen[j, q] for q in range(nr)], axis=1)
            l_high = lhs.astype(BF16)
            l_both = jnp.concatenate([lhs, lhs - l_high.astype(F32)], axis=0).astype(BF16)

            def tile(s, _):
                rows = pl.ds(pl.multiple_of(s * share, 8), share)
                rhs = jnp.concatenate(
                    [slab[rows, pl.ds(pl.multiple_of(q * quarter + j * CHUNK, CHUNK), CHUNK)]
                     for q in range(nr)], axis=1)
                r_high, r_low = split2(rhs)
                both = lax.dot_general(l_both, r_high, NT, preferred_element_type=F32)
                value = lax.dot_general(l_high, r_low, NT, preferred_element_type=F32)
                value += both[:sym] + both[sym:]
                acc[s // nd, lax.rem(s, nd)] += value
                return 0

            lax.fori_loop(0, nc * nd, tile, 0)

        return 0

    lax.fori_loop(0, units + PRODUCT_LAG, step, 0)

    live = blocks[d, r] >= 0
    acc[...] = jnp.where(live, acc[...], 0.0)

    def col_copy(o):
        to = lax.rem(c + o, nc)
        return remote(acc.at[to], got_col.at[o], col_send.at[o], col_recv.at[o], col=to)

    for o in range(1, nc):
        col_copy(o).start()
    for o in range(1, nc):
        col_copy(o).wait_recv()
    total = acc[c]
    for o in range(1, nc):
        total += got_col[o]
    got_col[0] = total

    def depth_copy(o):
        to = lax.rem(d + o, nd)
        return remote(got_col.at[0, to], got_depth.at[o], depth_send.at[o], depth_recv.at[o], depth=to)

    for o in range(1, nd):
        depth_copy(o).start()
    for o in range(1, nd):
        depth_copy(o).wait_recv()
    total = got_col[0, d]
    for o in range(1, nd):
        total += got_depth[o]

    back = spread_back[...].astype(BF16)
    high, low = split2(total)
    out[...] = (lax.dot_general(high, back, TN, preferred_element_type=F32)
                + lax.dot_general(low, back, TN, preferred_element_type=F32))

    for o in range(1, nc):
        col_copy(o).wait_send()
    for o in range(1, nd):
        depth_copy(o).wait_send()

    def finish(j, _):
        for o in range(1, nr):
            first_copy(j, o).wait_send()
            plane_copy(j, o).wait_send()
        return 0

    lax.fori_loop(0, steps, finish, 0)

    def finish_line(u, _):
        own_copy(u).wait_send()

        @pl.when(inner)
        def _():
            forward_copy(u).wait_send()
            joint_copy(u).wait_send()

        return 0

    lax.fori_loop(0, units, finish_line, 0)


def per_device(mesh, integrals, amplitudes, block_list, pair_list):
    nr, nc, nd = mesh.shape["row"], mesh.shape["col"], mesh.shape["depth"]
    _, rows, width = integrals.shape
    nblk, own_pairs, _ = amplitudes.shape
    pairs = pair_list.shape[0]
    nocc = int(round(pairs ** 0.5))
    sym = nocc * (nocc + 1) // 2
    plane_pairs = nr * own_pairs
    share = rows // (nc * nd)
    steps = width // nr // CHUNK
    units = steps * GROUPS

    dma = pltpu.SemaphoreType.DMA
    return pl.pallas_call(
        functools.partial(ladder_kernel, nr, nc, nd),
        out_shape=jax.ShapeDtypeStruct((share, pairs), F32),
        in_specs=[
            pl.BlockSpec(memory_space=pl.ANY),
            pl.BlockSpec(memory_space=pl.ANY),
            pl.BlockSpec(memory_space=pl.ANY),
            pl.BlockSpec(memory_space=pl.ANY),
        ],
        out_specs=pl.BlockSpec(memory_space=pltpu.VMEM),
        scratch_shapes=[
            pltpu.VMEM((2, pairs), jnp.int32),
            pltpu.SMEM(block_list.shape, jnp.int32),
            pltpu.VMEM((rows, width), F32),
            pltpu.VMEM((steps, nd, nblk, plane_pairs, CHUNK), F32),
            pltpu.VMEM((steps, nblk, sym, CHUNK), F32),
            pltpu.VMEM((steps, nr, sym, CHUNK), F32),
            pltpu.VMEM((steps, nr, sym, CHUNK), F32),
            pltpu.VMEM((nc, nd, sym, share), F32),
            pltpu.VMEM((nc, nd, sym, share), F32),
            pltpu.VMEM((nd, sym, share), F32),
            pltpu.VMEM((sym, pairs), F32),
            pltpu.VMEM((sym, plane_pairs), F32),
            pltpu.VMEM((sym, pairs), F32),
            dma, dma, dma, dma((steps, nr)), dma((steps, nr)),
            dma((units, 3)), dma((units, nd + 1)),
            dma((steps, nr)), dma((steps, nr)),
            dma((nc,)), dma((nc,)), dma((nd,)), dma((nd,)),
        ],
        compiler_params=pltpu.CompilerParams(
            collective_id=0, has_side_effects=True, vmem_limit_bytes=56 * 1024 * 1024
        ),
        cost_estimate=pl.CostEstimate(
            flops=6 * sym * rows * width, bytes_accessed=4 * rows * width, transcendentals=0
        ),
    )(pair_list.T, block_list, amplitudes, integrals).T


def solution(mesh):
    return jax.shard_map(
        functools.partial(per_device, mesh),
        mesh=mesh,
        in_specs=(
            P(("col", "depth"), "row", None),
            P("col", ("row", "depth"), None),
            P("col", None),
            P(),
        ),
        out_specs=P(None, ("row", "col", "depth")),
        check_vma=False,
    )
```

```python
import functools

import jax
import jax.numpy as jnp
from jax import lax
from jax.experimental import pallas as pl
from jax.experimental.pallas import tpu as pltpu
from jax.sharding import PartitionSpec as P

F32 = jnp.float32
BF16 = jnp.bfloat16
CHUNK = 128
GROUPS = 1
JOINT_LAG = 1
OUTER_LAG = 3
PRODUCT_LAG = 4
NT = (((1,), (1,)), ((), ()))
TN = (((0,), (0,)), ((), ()))


def split2(value):
    high = value.astype(BF16)
    return high, (value - high.astype(F32)).astype(BF16)


def dot(lhs, rhs):
    return jnp.dot(lhs, rhs, preferred_element_type=F32)


def ladder_kernel(
    nr, nc, nd,
    pair_list, block_list, amp, integ, out,
    pairs, blocks, slab, raw, joint, staged, chosen, acc, got_col, got_depth, mask_in, mask_ext, spread_back,
    pair_sem, block_sem, slab_sem, first_send, first_recv, line_send, line_recv, plane_send, plane_recv,
    col_send, col_recv, depth_send, depth_recv,
):
    r = lax.axis_index("row")
    c = lax.axis_index("col")
    d = lax.axis_index("depth")
    nblk, own_pairs, width = amp.shape
    quarter = width // nr
    steps = quarter // CHUNK
    plane_pairs = nr * own_pairs
    sym = mask_in.shape[0]
    share = out.shape[0]
    units = steps * GROUPS
    per_group = nblk // GROUPS

    def remote(src, dst, send, recv, **to):
        return pltpu.make_async_remote_copy(
            src_ref=src, dst_ref=dst, send_sem=send, recv_sem=recv,
            device_id=to, device_id_type=pl.DeviceIdType.MESH,
        )

    inner = jnp.logical_and(d >= 1, d <= 2)
    outer = jnp.logical_or(d == 0, d == 3)
    lower = d < 2
    ext = jnp.where(lower, 0, 3)
    mate = 3 - d
    inward = jnp.where(lower, d + 1, d - 1)
    outward = jnp.where(lower, 0, 3)

    barrier = pltpu.get_barrier_semaphore()
    for o in range(1, nr):
        pl.semaphore_signal(barrier, inc=1, device_id={"row": lax.rem(r + o, nr)},
                            device_id_type=pl.DeviceIdType.MESH)
    for o in range(1, nc):
        pl.semaphore_signal(barrier, inc=1, device_id={"col": lax.rem(c + o, nc)},
                            device_id_type=pl.DeviceIdType.MESH)
    for o in range(1, nd):
        pl.semaphore_signal(barrier, inc=1, device_id={"depth": lax.rem(d + o, nd)},
                            device_id_type=pl.DeviceIdType.MESH)
    slab_copy = pltpu.make_async_copy(integ.at[0], slab, slab_sem)
    pair_copy = pltpu.make_async_copy(pair_list, pairs, pair_sem)
    block_copy = pltpu.make_async_copy(block_list, blocks, block_sem)
    pair_copy.start()
    block_copy.start()
    pl.semaphore_wait(barrier, nr + nc + nd - 3)

    def first_copy(j, o):
        to = lax.rem(r + o, nr)
        at = pl.multiple_of(to * quarter + j * CHUNK, CHUNK)
        src = amp.at[:, :, pl.ds(at, CHUNK)]
        dst = raw.at[j, d, :, pl.ds(pl.multiple_of(r * own_pairs, own_pairs), own_pairs), :]
        if o == 0:
            return pltpu.make_async_copy(src, dst, first_recv.at[j, 0])
        return remote(src, dst, first_send.at[j, o], first_recv.at[j, o], row=to)

    def first_start(j, _):
        for o in range(nr):
            first_copy(j, o).start()
        return 0

    lax.fori_loop(0, 1, first_start, 0)

    pair_copy.wait()
    block_copy.wait()
    first, second = pairs[0:1, :], pairs[1:2, :]
    big, small = jnp.maximum(first, second), jnp.minimum(first, second)
    n = nd * plane_pairs
    hit = ((big * (big + 1)) >> 1) + small == lax.broadcasted_iota(jnp.int32, (n, n), 0)
    spread_back[...] = jnp.where(hit, 1.0, 0.0)[:sym]
    weighted = jnp.where(hit, jnp.where(big == small, 2.0, 1.0), 0.0).T
    planes = []
    for z in range(nd):
        planes.append(jnp.concatenate(
            [weighted[(q * nd + z) * own_pairs:(q * nd + z + 1) * own_pairs] for q in range(nr)], axis=0))
    none = jnp.zeros_like(planes[0])
    first_plane = jnp.where(lower, none, planes[0])
    last_plane = jnp.where(lower, planes[3], none)
    mask_in[...] = jnp.concatenate([first_plane, planes[1], planes[2], last_plane], axis=0).T[:sym]
    mask_ext[...] = jnp.concatenate([jnp.where(lower, planes[0], planes[3]), none], axis=0).T[:sym, :plane_pairs]
    acc[...] = jnp.zeros_like(acc)

    def part(ref, u, *at):
        return ref.at[(u // GROUPS, *at, pl.ds(lax.rem(u, GROUPS) * per_group, per_group))]

    def own_copy(u):
        return remote(part(raw, u, d), part(raw, u, d), line_send.at[u, 0], line_recv.at[u, d], depth=inward)

    def forward_copy(u):
        return remote(part(raw, u, outward), part(raw, u, outward), line_send.at[u, 1],
                      line_recv.at[u, outward], depth=inward)

    def joint_copy(u):
        return remote(part(joint, u), part(joint, u), line_send.at[u, 2], line_recv.at[u, nd], depth=outward)

    def raw_arrived(u, z):
        remote(part(raw, u, z), part(raw, u, z), line_send.at[u, 0], line_recv.at[u, z], depth=inward).wait_recv()

    def plane_copy(j, o):
        to = lax.rem(r + o, nr)
        return remote(staged.at[j, o], chosen.at[j, r], plane_send.at[j, o], plane_recv.at[j, o], row=to)

    def spread(j):
        m_ext = mask_ext[...].astype(BF16)
        sums = []
        for b in range(0, nblk, 2):
            high, low = split2(jnp.concatenate([raw[j, ext, b], raw[j, ext, b + 1]], axis=1))
            value = dot(m_ext, high) + dot(m_ext, low)
            sums.append(joint[j, b] + value[:, :CHUNK])
            sums.append(joint[j, b + 1] + value[:, CHUNK:])
        for o in range(nr):
            to = lax.rem(r + o, nr)
            at = lax.rem(jnp.maximum(blocks[d, to], 0), nblk)
            picked = sums[0]
            for b in range(1, nblk):
                picked = jnp.where(at == b, sums[b], picked)
            if o == 0:
                chosen[j, r] = picked
            else:
                staged[j, o] = picked
                plane_copy(j, o).start()

    def step(t, _):
        @pl.when(t + 1 < steps)
        def _():
            first_start(t + 1, 0)

        @pl.when(t == 1)
        def _():
            slab_copy.start()

        @pl.when(t < units)
        def _():
            @pl.when(lax.rem(t, GROUPS) == 0)
            def _():
                for o in range(nr):
                    copy = first_copy(t // GROUPS, o)
                    if o == 0:
                        copy.wait()
                    else:
                        copy.wait_recv()

            own_copy(t).start()

        @pl.when(jnp.logical_and(inner, t < units))
        def _():
            raw_arrived(t, outward)
            forward_copy(t).start()

        @pl.when(jnp.logical_and(inner, jnp.logical_and(t >= JOINT_LAG, t < units + JOINT_LAG)))
        def _():
            u = t - JOINT_LAG
            j = u // GROUPS
            raw_arrived(u, mate)
            raw_arrived(u, 3 - outward)
            m_in = mask_in[...].astype(BF16)
            for k in range(0, per_group, 2):
                b = lax.rem(u, GROUPS) * per_group + k
                high, low = split2(jnp.concatenate(
                    [raw[j, :, b + e].reshape(nd * plane_pairs, CHUNK) for e in range(2)], axis=1))
                value = dot(m_in, high) + dot(m_in, low)
                joint[j, b] = value[:, :CHUNK]
                joint[j, b + 1] = value[:, CHUNK:]
            joint_copy(u).start()

            @pl.when(lax.rem(u, GROUPS) == GROUPS - 1)
            def _():
                spread(j)

        @pl.when(jnp.logical_and(outer, jnp.logical_and(t >= OUTER_LAG, t < units + OUTER_LAG)))
        def _():
            u = t - OUTER_LAG
            joint_copy(u).wait_recv()

            @pl.when(lax.rem(u, GROUPS) == GROUPS - 1)
            def _():
                spread(u // GROUPS)

        @pl.when(t == PRODUCT_LAG)
        def _():
            slab_copy.wait()

        @pl.when(jnp.logical_and(t >= PRODUCT_LAG, lax.rem(t - PRODUCT_LAG, GROUPS) == GROUPS - 1))
        def _():
            j = (t - PRODUCT_LAG) // GROUPS
            for o in range(1, nr):
                plane_copy(j, o).wait_recv()
            lhs = jnp.concatenate([chosen[j, q] for q in range(nr)], axis=1)
            l_high = lhs.astype(BF16)
            l_both = jnp.concatenate([lhs, lhs - l_high.astype(F32)], axis=0).astype(BF16)

            def tile(s, _):
                rows = pl.ds(pl.multiple_of(s * share, 8), share)
                rhs = jnp.concatenate(
                    [slab[rows, pl.ds(pl.multiple_of(q * quarter + j * CHUNK, CHUNK), CHUNK)]
                     for q in range(nr)], axis=1)
                r_high, r_low = split2(rhs)
                both = lax.dot_general(l_both, r_high, NT, preferred_element_type=F32)
                value = lax.dot_general(l_high, r_low, NT, preferred_element_type=F32)
                value += both[:sym] + both[sym:]
                acc[s // nd, lax.rem(s, nd)] += value
                return 0

            lax.fori_loop(0, nc * nd, tile, 0, unroll=min(4, nc * nd))

        return 0

    lax.fori_loop(0, units + PRODUCT_LAG, step, 0)

    live = blocks[d, r] >= 0
    acc[...] = jnp.where(live, acc[...], 0.0)

    def col_copy(o):
        to = lax.rem(c + o, nc)
        return remote(acc.at[to], got_col.at[o], col_send.at[o], col_recv.at[o], col=to)

    for o in range(1, nc):
        col_copy(o).start()
    for o in range(1, nc):
        col_copy(o).wait_recv()
    total = acc[c]
    for o in range(1, nc):
        total += got_col[o]
    got_col[0] = total

    def depth_copy(o):
        to = lax.rem(d + o, nd)
        return remote(got_col.at[0, to], got_depth.at[o], depth_send.at[o], depth_recv.at[o], depth=to)

    for o in range(1, nd):
        depth_copy(o).start()
    for o in range(1, nd):
        depth_copy(o).wait_recv()
    total = got_col[0, d]
    for o in range(1, nd):
        total += got_depth[o]

    back = spread_back[...].astype(BF16)
    high, low = split2(total)
    out[...] = (lax.dot_general(high, back, TN, preferred_element_type=F32)
                + lax.dot_general(low, back, TN, preferred_element_type=F32))

    for o in range(1, nc):
        col_copy(o).wait_send()
    for o in range(1, nd):
        depth_copy(o).wait_send()

    def finish(j, _):
        for o in range(1, nr):
            first_copy(j, o).wait_send()
            plane_copy(j, o).wait_send()
        return 0

    lax.fori_loop(0, steps, finish, 0)

    def finish_line(u, _):
        own_copy(u).wait_send()

        @pl.when(inner)
        def _():
            forward_copy(u).wait_send()
            joint_copy(u).wait_send()

        return 0

    lax.fori_loop(0, units, finish_line, 0)


def per_device(mesh, integrals, amplitudes, block_list, pair_list):
    nr, nc, nd = mesh.shape["row"], mesh.shape["col"], mesh.shape["depth"]
    _, rows, width = integrals.shape
    nblk, own_pairs, _ = amplitudes.shape
    pairs = pair_list.shape[0]
    nocc = int(round(pairs ** 0.5))
    sym = nocc * (nocc + 1) // 2
    plane_pairs = nr * own_pairs
    share = rows // (nc * nd)
    steps = width // nr // CHUNK
    units = steps * GROUPS

    dma = pltpu.SemaphoreType.DMA
    return pl.pallas_call(
        functools.partial(ladder_kernel, nr, nc, nd),
        out_shape=jax.ShapeDtypeStruct((share, pairs), F32),
        in_specs=[
            pl.BlockSpec(memory_space=pl.ANY),
            pl.BlockSpec(memory_space=pl.ANY),
            pl.BlockSpec(memory_space=pl.ANY),
            pl.BlockSpec(memory_space=pl.ANY),
        ],
        out_specs=pl.BlockSpec(memory_space=pltpu.VMEM),
        scratch_shapes=[
            pltpu.VMEM((2, pairs), jnp.int32),
            pltpu.SMEM(block_list.shape, jnp.int32),
            pltpu.VMEM((rows, width), F32),
            pltpu.VMEM((steps, nd, nblk, plane_pairs, CHUNK), F32),
            pltpu.VMEM((steps, nblk, sym, CHUNK), F32),
            pltpu.VMEM((steps, nr, sym, CHUNK), F32),
            pltpu.VMEM((steps, nr, sym, CHUNK), F32),
            pltpu.VMEM((nc, nd, sym, share), F32),
            pltpu.VMEM((nc, nd, sym, share), F32),
            pltpu.VMEM((nd, sym, share), F32),
            pltpu.VMEM((sym, pairs), F32),
            pltpu.VMEM((sym, plane_pairs), F32),
            pltpu.VMEM((sym, pairs), F32),
            dma, dma, dma, dma((steps, nr)), dma((steps, nr)),
            dma((units, 3)), dma((units, nd + 1)),
            dma((steps, nr)), dma((steps, nr)),
            dma((nc,)), dma((nc,)), dma((nd,)), dma((nd,)),
        ],
        compiler_params=pltpu.CompilerParams(
            collective_id=0, has_side_effects=True, vmem_limit_bytes=56 * 1024 * 1024
        ),
        cost_estimate=pl.CostEstimate(
            flops=6 * sym * rows * width, bytes_accessed=4 * rows * width, transcendentals=0
        ),
    )(pair_list.T, block_list, amplitudes, integrals).T


def solution(mesh):
    return jax.shard_map(
        functools.partial(per_device, mesh),
        mesh=mesh,
        in_specs=(
            P(("col", "depth"), "row", None),
            P("col", ("row", "depth"), None),
            P("col", None),
            P(),
        ),
        out_specs=P(None, ("row", "col", "depth")),
        check_vma=False,
    )
```
